512 devices in a mesh: grp: 16 (over y, z_lo), dev: 32 (over z_hi, x, core).
Axes of the slice: x: 4, y: 4, z: 16 (z_hi: 4, z_lo: 4; z = z_hi * 4 + z_lo), core: 2. Of those that a mesh axis runs over, the one named last changes fastest.
Arguments:
- queries: bfloat16 [4096, 4096], P('dev', 'grp'), may hold values from -16 to 16
- passages: bfloat16 [8192, 4096], P('dev', 'grp'), may hold values from -8 to 8
- positive: int32 [4096], P('dev'), may hold values from 0 to 4095, each once
Outputs:
- query_grad: bfloat16 [4096, 4096], P('dev', 'grp')
- passage_grad: bfloat16 [8192, 4096], P('dev', 'grp')
The draws below stay inside these ranges and needn't reach their ends.
Inputs may be any that keep to these rules, and one draw needn't show every extreme that they name: Every one of the first 4096 passages is the positive of exactly one query.
All inputs are finite; a program needn't handle non-finite values.
Results may differ from the reference program's by a relative error of at most 0.0035.
Values may be sent and summed in bfloat16 or wider, within the bound.
No kernel may reach another device: no remote copies, remote signals or barrier semaphores. Data moves between devices by JAX's collectives and lax.ppermute only.
A program may use at most 64 MiB of HBM per device.

```python
import math
import jax
import jax.numpy as jnp
from jax import lax

D = 4096
BATCH = 4096


def planted_rows(key):
    chosen = max(4, BATCH // 32)
    side = 1.0
    while side * side * 4.0 < 300.0 / math.sqrt(D):
        side = 2.0
    row_pick = jax.random.permutation(jax.random.fold_in(key, 11), BATCH)[:chosen].astype(jnp.int32)
    col_pick = jax.random.permutation(jax.random.fold_in(key, 12), 2 * BATCH)[:2 * chosen].astype(jnp.int32)
    first_cols = col_pick[:chosen]
    second_cols = col_pick[chosen:]
    first_signs = 2.0 * jax.random.randint(jax.random.fold_in(key, 13), (chosen, D), 0, 2).astype(jnp.float32) - 1.0
    second_signs = 2.0 * jax.random.randint(jax.random.fold_in(key, 14), (chosen, D), 0, 2).astype(jnp.float32) - 1.0
    parity = (jnp.arange(chosen, dtype=jnp.int32) % 2).astype(jnp.float32)
    shrink = 1.0 - (1.0 + parity) / 256.0
    strong_gap = jax.random.uniform(jax.random.fold_in(key, 15), (chosen,), jnp.float32, 2.0, 2.6)
    milder_gap = jax.random.uniform(jax.random.fold_in(key, 16), (chosen,), jnp.float32, 1.7, 2.3)
    gap_size = jnp.where(parity > 0.5, milder_gap, strong_gap)
    target = gap_size / (1.0 - shrink * shrink)
    strength = target / (2.0 * math.sqrt(D))
    first_rows = side * first_signs
    second_rows = (side * shrink)[:, None] * second_signs
    query_rows = (strength / (side * side))[:, None] * (first_rows + second_rows)
    return (row_pick, first_cols, second_cols, first_rows, second_rows, query_rows)


def draw_queries(key, part):
    row_pick, first_cols, second_cols, first_rows, second_rows, query_rows = planted_rows(key)
    key = jax.random.fold_in(key, 1)
    base = jax.random.truncated_normal(jax.random.fold_in(key, 3), -6.0, 6.0, (BATCH, D), jnp.float32)
    return base.at[row_pick].set(query_rows).astype(jnp.bfloat16)


def draw_passages(key, part):
    row_pick, first_cols, second_cols, first_rows, second_rows, query_rows = planted_rows(key)
    key = jax.random.fold_in(key, 2)
    base = jax.random.truncated_normal(jax.random.fold_in(key, 4), -6.0, 6.0, (2 * BATCH, D), jnp.float32)
    base = base.at[first_cols].set(first_rows)
    base = base.at[second_cols].set(second_rows)
    return base.astype(jnp.bfloat16)


def setup_inputs(seed: int = 0) -> dict:
    keys = jax.random.split(jax.random.key(seed), 4)
    return {
        "queries": draw_queries(jax.random.fold_in(keys[3], 71), 0),
        "passages": draw_passages(jax.random.fold_in(keys[3], 71), 0),
        "positive": jax.random.permutation(keys[2], BATCH).astype(jnp.int32),
    }


def reference(queries, passages, positive):
    scale = 2.0 / math.sqrt(D)
    logits = scale * jnp.dot(queries, passages.T, preferred_element_type=jnp.float32)
    top = lax.optimization_barrier(jnp.max(logits, axis=1, keepdims=True))
    exps = jnp.exp(logits - top)
    prob = exps / lax.optimization_barrier(jnp.sum(exps, axis=1, keepdims=True))
    columns = jnp.arange(2 * BATCH, dtype=jnp.int32)
    onehot = (columns[None, :] == positive[:, None]).astype(jnp.float32)
    weights = (prob - onehot).astype(jnp.bfloat16)
    query_grad = jnp.dot(weights, passages, preferred_element_type=jnp.float32).astype(jnp.bfloat16)
    passage_grad = jnp.dot(weights.T, queries, preferred_element_type=jnp.float32).astype(jnp.bfloat16)
    return (query_grad, passage_grad)
```

```python
import math

import jax
import jax.numpy as jnp
from jax import lax
from jax.sharding import Mesh, PartitionSpec as P

ROWS = ("zh", "x", "c")
FEATS = ("y", "zl")
BF = jnp.bfloat16
F32 = jnp.float32


def shift(value, axis, step):
    n = lax.axis_size(axis)
    return lax.ppermute(value, axis, [(i, (i + step) % n) for i in range(n)])


def gather(value, axis, dim):
    n = lax.axis_size(axis)
    me = lax.axis_index(axis)
    size = value.shape[dim]
    whole = list(value.shape)
    whole[dim] = size * n
    out = jnp.zeros(whole, value.dtype)
    for step in range(n):
        block = value if step == 0 else shift(value, axis, step)
        out = lax.dynamic_update_slice_in_dim(out, block, ((me - step) % n) * size, dim)
    return out


def scatter_sum(piece, axis):
    n = lax.axis_size(axis)
    me = lax.axis_index(axis)
    moved = [shift(piece((me + step) % n).astype(BF), axis, step) for step in range(1, n)]
    total = piece(me)
    for block in moved:
        total = total + block.astype(F32)
    return total


def dot(a, b, over_a, over_b):
    return lax.dot_general(a, b, (((over_a,), (over_b,)), ((), ())), preferred_element_type=F32)


def per_device(queries, passages, positive):
    rows, width = queries.shape
    groups = lax.axis_size(FEATS)
    devs = lax.axis_size(ROWS)
    full = width * groups
    part = rows // groups
    scale = 2.0 / math.sqrt(full)
    core, x, y = lax.axis_index("c"), lax.axis_index("x"), lax.axis_index("y")
    group = lax.axis_index(FEATS)
    dev = lax.axis_index(ROWS)

    mine = lax.all_to_all(queries.reshape(groups, part, width), FEATS, 0, 0, tiled=True)
    mine = mine.transpose(1, 0, 2).reshape(part, full)
    half = gather(gather(mine, "zh", 0), "x", 0)
    q = gather(half, "c", 0)

    p = gather(gather(passages, "zl", 1), "y", 1)
    count = p.shape[0]

    logits = dot(q, p, 1, 1) * scale
    n_q = logits.shape[0]
    top = jnp.max(logits, axis=1)
    exps = jnp.exp(logits - top[:, None])
    total = jnp.sum(exps, axis=1)
    own_pos = lax.dynamic_slice_in_dim(positive, group * part, part).astype(F32)
    note = jnp.concatenate([top, total, jnp.pad(own_pos, (0, 128 - part))])
    notes = lax.all_to_all(
        jnp.broadcast_to(note, (devs, note.shape[0])), ("c", "x", "zh"), 0, 0, tiled=True
    )
    tops, totals = notes[:, :n_q], notes[:, n_q : 2 * n_q]
    pos = notes[:, 2 * n_q : 2 * n_q + part].reshape(n_q).astype(jnp.int32)
    peak = jnp.max(tops, axis=0)
    denom = jnp.sum(totals * jnp.exp(tops - peak), axis=0)
    factor = jnp.exp(top - peak) / denom
    columns = lax.broadcasted_iota(jnp.int32, (n_q, count), 1) + dev * count
    onehot = (columns == pos[:, None]).astype(F32)
    weights = (exps * factor[:, None] - onehot).astype(BF)

    strip = full // lax.axis_size("y")

    def passage_piece(owner):
        return dot(weights, lax.dynamic_slice_in_dim(q, owner * strip, strip, 1), 0, 0)

    by_y = scatter_sum(passage_piece, "y")
    passage_grad = scatter_sum(lambda owner: lax.dynamic_slice_in_dim(by_y, owner * width, width, 1), "zl")

    n_half = n_q // 2
    p_other = shift(p, "c", 1)
    w_mine = lax.dynamic_slice_in_dim(weights, core * n_half, n_half, 0)
    w_other = shift(lax.dynamic_slice_in_dim(weights, (1 - core) * n_half, n_half, 0), "c", 1)
    chip = dot(w_mine, p, 1, 0) + dot(w_other, p_other, 1, 0)
    n_x = n_half // lax.axis_size("x")
    by_x = scatter_sum(lambda owner: lax.dynamic_slice_in_dim(chip, owner * n_x, n_x, 0), "x")
    by_zh = scatter_sum(lambda owner: lax.dynamic_slice_in_dim(by_x, owner * part, part, 0), "zh")
    back = by_zh.astype(BF).reshape(part, groups, width).transpose(1, 0, 2)
    query_grad = lax.all_to_all(back, FEATS, 0, 0, tiled=True).reshape(rows, width)
    return query_grad, passage_grad.astype(BF)


def solution(mesh):
    fine = Mesh(mesh.devices.reshape(4, 4, 4, 4, 2), FEATS + ROWS)
    in_specs = (P(ROWS, FEATS), P(ROWS, FEATS), P(ROWS))
    out_specs = (P(ROWS, FEATS), P(ROWS, FEATS))
    return jax.shard_map(per_device, mesh=fine, in_specs=in_specs, out_specs=out_specs, check_vma=False)
```

```python
import math

import jax
import jax.numpy as jnp
from jax import lax
from jax.experimental import pallas as pl
from jax.experimental.pallas import tpu as pltpu
from jax.sharding import Mesh, PartitionSpec as P

ROWS = ("zh", "x", "c")
FEATS = ("y", "zl")
COLUMN = ("zh", "zl")
BF = jnp.bfloat16
F32 = jnp.float32


def shift(value, axis, step):
    n = lax.axis_size(axis)
    return lax.ppermute(value, axis, [(i, (i + step) % n) for i in range(n)])


def exchange(blocks, axis):
    return lax.all_to_all(blocks, axis, 0, 0, tiled=True)


def gather(value, axis):
    n = lax.axis_size(axis)
    return exchange(jnp.broadcast_to(value, (n, *value.shape)), axis)


def dot(a, b, over_a, over_b):
    return lax.dot_general(a, b, (((over_a,), (over_b,)), ((), ())), preferred_element_type=F32)


def call(kernel, outs, flops, place, *arrays):
    size = sum(a.size * a.dtype.itemsize for a in (*arrays, *outs))
    return pl.pallas_call(
        kernel,
        out_shape=outs,
        in_specs=[pl.BlockSpec(memory_space=pltpu.SMEM)] + [pl.BlockSpec(memory_space=pltpu.VMEM)] * len(arrays),
        out_specs=[pl.BlockSpec(memory_space=pltpu.VMEM)] * len(outs),
        cost_estimate=pl.CostEstimate(flops=flops, bytes_accessed=size, transcendentals=0),
        compiler_params=pltpu.CompilerParams(vmem_limit_bytes=32 * 2**20),
    )(place.reshape(1), *arrays)


def in_x_order(w_ref, half):
    n_zh, _, n_x = w_ref.shape[:3]
    return jnp.concatenate([w_ref[z, half, x] for x in range(n_x) for z in range(n_zh)], axis=0)


def passage_kernel(zl_ref, w_ref, near_ref, far_ref, own_ref, send_ref):
    n_zl, width = send_ref.shape[0] + 1, own_ref.shape[1]
    w_near, w_far = in_x_order(w_ref, 0), in_x_order(w_ref, 1)
    for t in range(n_zl):
        at = pl.ds(pl.multiple_of((zl_ref[0] + t) % n_zl * width, width), width)
        block = dot(w_near, near_ref[:, at], 0, 0) + dot(w_far, far_ref[:, at], 0, 0)
        if t == 0:
            own_ref[...] = block
        else:
            send_ref[t - 1] = block.astype(BF)


def query_kernel(x_ref, w_ref, other_ref, p_ref, p_other_ref, own_ref, send_ref):
    n_zh, _, n_x = w_ref.shape[:3]
    for x in range(n_x):
        mine = jnp.concatenate([w_ref[z, 0, x] for z in range(n_zh)], axis=0)
        theirs = jnp.concatenate([other_ref[z, x] for z in range(n_zh)], axis=0)
        block = dot(mine, p_ref[...], 1, 0) + dot(theirs, p_other_ref[...], 1, 0)
        send_ref[x] = block.astype(BF)

        @pl.when(x_ref[0] == x)
        def _():
            own_ref[...] = block


def total_kernel(x_ref, own_ref, moved_ref, out_ref):
    n_x = moved_ref.shape[0]
    n_blocks, band, width = out_ref.shape
    n_zl = own_ref.shape[1] // width
    for z in range(n_blocks // n_zl):
        rows = pl.ds(z * band, band)
        total = own_ref[rows, :]
        for x in range(n_x):
            total = total + jnp.where(x_ref[0] == x, 0.0, moved_ref[x, rows, :].astype(F32))
        for l in range(n_zl):
            out_ref[z * n_zl + l] = total[:, l * width : (l + 1) * width].astype(BF)


def per_device(queries, passages, positive):
    rows, width = queries.shape
    count = passages.shape[0]
    n_x, n_y, n_zh, n_zl = (lax.axis_size(a) for a in ("x", "y", "zh", "zl"))
    assert n_zh == n_y
    devs = lax.axis_size(ROWS)
    strip = width * n_zl
    scale = 2.0 / math.sqrt(strip * n_y)
    band = rows // n_zl
    n_q = 2 * n_x * band
    n_half = band * n_zh * n_x
    core, x, y, zl = (lax.axis_index(a) for a in ("c", "x", "y", "zl"))
    dev = lax.axis_index(ROWS)

    bands = jnp.broadcast_to(queries.reshape(n_zl, band, width), (n_zh, n_zl, band, width))
    mine = exchange(bands.reshape(n_zh * n_zl, band, width), COLUMN).reshape(n_zh, n_zl, band, width)
    mine = mine.transpose(0, 2, 1, 3).reshape(n_zh * band, strip)
    near = gather(mine, "x").reshape(n_half, strip)

    p = jnp.zeros((count, strip), BF)
    for t in range(n_zl):
        block = passages if t == 0 else shift(passages, "zl", t)
        p = lax.dynamic_update_slice_in_dim(p, block, (zl - t) % n_zl * width, 1)
    near, p = lax.optimization_barrier((near, p))
    far = shift(near, "c", 1)
    p_other = shift(p, "c", 1)

    partial = jnp.stack([dot(near, p, 1, 1), dot(far, p, 1, 1)])
    partial = partial.reshape(2 * n_x, n_zh, band, count).transpose(1, 0, 2, 3)
    moved = exchange(partial.reshape(n_y, n_q, count), "y")
    logits = moved[0]
    for i in range(1, n_y):
        logits = logits + moved[i]
    logits = logits * scale

    top = jnp.max(logits, axis=1)
    exps = jnp.exp(logits - top[:, None])
    total = jnp.sum(exps, axis=1)

    def flip_cores(row_values):
        return jnp.where(core == 0, row_values, jnp.roll(row_values, n_q // 2))

    own_pos = lax.dynamic_slice_in_dim(positive, zl * band, band).astype(F32)
    note = jnp.concatenate([flip_cores(top), flip_cores(total), jnp.pad(own_pos, (0, 128 - band))])
    notes = exchange(jnp.broadcast_to(note, (devs, note.shape[0])), ("c", "x", "zh"))
    tops, totals = notes[:, :n_q], notes[:, n_q : 2 * n_q]
    pos = notes[:, 2 * n_q : 2 * n_q + band].reshape(2 * n_x, n_zh, band)
    pos = lax.dynamic_index_in_dim(pos, y, 1, keepdims=False).reshape(n_q).astype(jnp.int32)
    peak = jnp.max(tops, axis=0)
    denom = jnp.sum(totals * jnp.exp(tops - peak), axis=0)
    factor = jnp.exp(top - flip_cores(peak)) / flip_cores(denom)
    columns = lax.broadcasted_iota(jnp.int32, (n_q, count), 1) + dev * count
    onehot = (columns == flip_cores(pos)[:, None]).astype(F32)
    weights = (exps * factor[:, None] - onehot).astype(BF)
    weights = gather(weights, "y").reshape(n_zh, 2, n_x, band, count)
    w_other = shift(weights[:, 1], "c", 1)

    flops = 4 * n_half * count * strip
    by_x, chip = call(
        query_kernel,
        [jax.ShapeDtypeStruct((n_zh * band, strip), F32), jax.ShapeDtypeStruct((n_x, n_zh * band, strip), BF)],
        flops, x, weights, w_other, p, p_other,
    )
    moved = exchange(chip, "x")
    (back,) = call(
        total_kernel, [jax.ShapeDtypeStruct((n_zh * n_zl, band, width), BF)], 0, x, by_x, moved
    )

    passage_grad, ahead = call(
        passage_kernel,
        [jax.ShapeDtypeStruct((count, width), F32), jax.ShapeDtypeStruct((n_zl - 1, count, width), BF)],
        flops, zl, weights, near, far,
    )
    for t in range(1, n_zl):
        passage_grad = passage_grad + shift(ahead[t - 1], "zl", t).astype(F32)
    back, passage_grad = lax.optimization_barrier((back, passage_grad))

    back = exchange(back, COLUMN).reshape(n_zh, rows, width)
    query_grad = jnp.sum(back.astype(F32), axis=0)
    return query_grad.astype(BF), passage_grad.astype(BF)


def solution(mesh):
    fine = Mesh(mesh.devices.reshape(4, 4, 4, 4, 2), FEATS + ROWS)
    in_specs = (P(ROWS, FEATS), P(ROWS, FEATS), P(ROWS))
    out_specs = (P(ROWS, FEATS), P(ROWS, FEATS))
    return jax.shard_map(per_device, mesh=fine, in_specs=in_specs, out_specs=out_specs, check_vma=False)
```

```python
import math

import jax
import jax.numpy as jnp
from jax import lax
from jax.experimental import pallas as pl
from jax.experimental.pallas import tpu as pltpu
from jax.sharding import Mesh, PartitionSpec as P

ROWS = ("zh", "x", "c")
FEATS = ("y", "zl")
COLUMN = ("zh", "zl")
BF = jnp.bfloat16
F32 = jnp.float32
BAND = 32


def shift(value, axis, step):
    n = lax.axis_size(axis)
    return lax.ppermute(value, axis, [(i, (i + step) % n) for i in range(n)])


def exchange(blocks, axis):
    return lax.all_to_all(blocks, axis, 0, 0, tiled=True)


def gather(value, axis):
    n = lax.axis_size(axis)
    return exchange(jnp.broadcast_to(value, (n, *value.shape)), axis)


def dot(a, b, over_a, over_b):
    return lax.dot_general(a, b, (((over_a,), (over_b,)), ((), ())), preferred_element_type=F32)


def call(kernel, outs, flops, place, *arrays, out_space=pltpu.VMEM, scratch=()):
    size = sum(a.size * a.dtype.itemsize for a in (*arrays, *outs))
    return pl.pallas_call(
        kernel,
        out_shape=outs,
        in_specs=[pl.BlockSpec(memory_space=pltpu.SMEM)] + [pl.BlockSpec(memory_space=pltpu.VMEM)] * len(arrays),
        out_specs=[pl.BlockSpec(memory_space=out_space)] * len(outs),
        scratch_shapes=list(scratch),
        cost_estimate=pl.CostEstimate(flops=flops, bytes_accessed=size, transcendentals=0),
        compiler_params=pltpu.CompilerParams(vmem_limit_bytes=32 * 2**20),
    )(place.reshape(1), *arrays)


def logits_kernel(place_ref, q_ref, p_ref, p_other_ref, out_ref):
    del place_ref
    n_zh, block, _ = out_ref.shape
    count = p_ref.shape[0]
    n_x = q_ref.shape[0] // n_zh // BAND
    for z in range(n_zh):
        rows = [q_ref[pl.ds((x * n_zh + z) * BAND, BAND), :] for x in range(n_x)]
        rows = jnp.concatenate(rows, axis=0)
        out_ref[z, :, :count] = dot(rows, p_ref[...], 1, 1)
        out_ref[z, :, count:] = dot(rows, p_other_ref[...], 1, 1)


def passage_kernel(zl_ref, w_ref, far_w_ref, near_ref, far_ref, own_ref, send_ref):
    n_zl, width, count = send_ref.shape[0] + 1, own_ref.shape[1], own_ref.shape[0]
    n_zh, n_x = w_ref.shape[:2]
    order = [(z, x) for x in range(n_x) for z in range(n_zh)]
    w_near = jnp.concatenate([w_ref[z, x, :, :count] for z, x in order], axis=0)
    w_far = jnp.concatenate([far_w_ref[z, x] for z, x in order], axis=0)
    for t in range(n_zl):
        at = pl.ds(pl.multiple_of((zl_ref[0] + t) % n_zl * width, width), width)
        block = dot(w_near, near_ref[:, at], 0, 0) + dot(w_far, far_ref[:, at], 0, 0)
        if t == 0:
            own_ref[...] = block
        else:
            send_ref[t - 1] = block.astype(BF)


def query_kernel(x_ref, w_ref, p_ref, p_other_ref, own_ref, send_ref, own, blocks, sems):
    n_zh, n_x = w_ref.shape[:2]
    count = p_ref.shape[0]
    copies = []
    for x in range(n_x):
        rows = jnp.concatenate([w_ref[z, x] for z in range(n_zh)], axis=0)
        block = dot(rows[:, :count], p_ref[...], 1, 0) + dot(rows[:, count:], p_other_ref[...], 1, 0)
        blocks[x] = block.astype(BF)
        copies.append(pltpu.make_async_copy(blocks.at[x], send_ref.at[x], sems.at[x]))
        copies[-1].start()

        @pl.when(x_ref[0] == x)
        def _():
            own[...] = block

    copies.append(pltpu.make_async_copy(own, own_ref, sems.at[n_x]))
    copies[-1].start()
    for copy in copies:
        copy.wait()


def total_kernel(x_ref, own_ref, moved_ref, out_ref):
    n_x = moved_ref.shape[0]
    n_blocks, band, width = out_ref.shape
    n_zl = own_ref.shape[1] // width
    for z in range(n_blocks // n_zl):
        rows = pl.ds(z * band, band)
        total = own_ref[rows, :]
        for x in range(n_x):
            total = total + jnp.where(x_ref[0] == x, 0.0, moved_ref[x, rows, :].astype(F32))
        for l in range(n_zl):
            out_ref[z * n_zl + l] = total[:, l * width : (l + 1) * width].astype(BF)


def per_device(queries, passages, positive):
    rows, width = queries.shape
    count = passages.shape[0]
    n_x, n_y, n_zh, n_zl = (lax.axis_size(a) for a in ("x", "y", "zh", "zl"))
    strip = width * n_zl
    scale = 2.0 / math.sqrt(strip * n_y)
    band = rows // n_zl
    assert n_zh == n_y and band == BAND
    n_q = n_x * band
    n_half = band * n_zh * n_x
    x, y, zl = (lax.axis_index(a) for a in ("x", "y", "zl"))
    dev = lax.axis_index(ROWS)

    bands = jnp.broadcast_to(queries.reshape(n_zl, band, width), (n_zh, n_zl, band, width))
    mine = exchange(bands.reshape(n_zh * n_zl, band, width), COLUMN).reshape(n_zh, n_zl, band, width)
    mine = mine.transpose(0, 2, 1, 3).reshape(n_zh * band, strip)
    near = gather(mine, "x").reshape(n_half, strip)

    p = jnp.zeros((count, strip), BF)
    for t in range(n_zl):
        block = passages if t == 0 else shift(passages, "zl", t)
        p = lax.dynamic_update_slice_in_dim(p, block, (zl - t) % n_zl * width, 1)
    p_other = shift(p, "c", 1)
    near, p = lax.optimization_barrier((near, p))
    far = shift(near, "c", 1)

    flops = 4 * n_half * count * strip
    (partial,) = call(
        logits_kernel, [jax.ShapeDtypeStruct((n_zh, n_q, 2 * count), F32)], flops, x, near, p, p_other
    )
    moved = exchange(partial, "y")
    logits = moved[0]
    for i in range(1, n_y):
        logits = logits + moved[i]
    logits = logits * scale

    top = jnp.max(logits, axis=1)
    exps = jnp.exp(logits - top[:, None])
    total = jnp.sum(exps, axis=1)
    own_pos = lax.dynamic_slice_in_dim(positive, zl * band, band).astype(F32)
    note = jnp.concatenate([top, total, jnp.pad(own_pos, (0, 128 - band))])
    notes = exchange(jnp.broadcast_to(note, (n_x * n_zh, note.shape[0])), ("x", "zh"))
    tops, totals = notes[:, :n_q], notes[:, n_q : 2 * n_q]
    pos = notes[:, 2 * n_q : 2 * n_q + band].reshape(n_x, n_zh, band)
    pos = lax.dynamic_index_in_dim(pos, y, 1, keepdims=False).reshape(n_q).astype(jnp.int32)
    peak = jnp.max(tops, axis=0)
    denom = jnp.sum(totals * jnp.exp(tops - peak), axis=0)
    factor = jnp.exp(top - peak) / denom
    columns = lax.broadcasted_iota(jnp.int32, (n_q, 2 * count), 1)
    columns = jnp.where(columns < count, columns + dev * count, columns - count + (dev ^ 1) * count)
    onehot = (columns == pos[:, None]).astype(F32)
    weights = (exps * factor[:, None] - onehot).astype(BF)
    weights = gather(weights, "y").reshape(n_zh, n_x, band, 2 * count)
    far_weights = shift(weights[..., count:], "c", 1)

    block = (n_zh * band, strip)
    by_x, chip = call(
        query_kernel,
        [jax.ShapeDtypeStruct(block, F32), jax.ShapeDtypeStruct((n_x, *block), BF)],
        flops, x, weights, p, p_other,
        out_space=pltpu.HBM,
        scratch=[pltpu.VMEM(block, F32), pltpu.VMEM((n_x, *block), BF), pltpu.SemaphoreType.DMA((n_x + 1,))],
    )
    moved = exchange(chip, "x")
    (back,) = call(
        total_kernel, [jax.ShapeDtypeStruct((n_zh * n_zl, band, width), BF)], 0, x, by_x, moved
    )

    passage_grad, ahead = call(
        passage_kernel,
        [jax.ShapeDtypeStruct((count, width), F32), jax.ShapeDtypeStruct((n_zl - 1, count, width), BF)],
        flops, zl, weights, far_weights, near, far,
    )
    arrived = [shift(ahead[t - 1], "zl", t) for t in range(1, n_zl)]
    back, arrived[0] = lax.optimization_barrier((back, arrived[0]))
    for block in arrived:
        passage_grad = passage_grad + block.astype(F32)

    back = exchange(back, COLUMN).reshape(n_zh, rows, width)
    query_grad = jnp.sum(back.astype(F32), axis=0)
    return query_grad.astype(BF), passage_grad.astype(BF)


def solution(mesh):
    fine = Mesh(mesh.devices.reshape(4, 4, 4, 4, 2), FEATS + ROWS)
    in_specs = (P(ROWS, FEATS), P(ROWS, FEATS), P(ROWS))
    out_specs = (P(ROWS, FEATS), P(ROWS, FEATS))
    return jax.shard_map(per_device, mesh=fine, in_specs=in_specs, out_specs=out_specs, check_vma=False)
```

```python
import math

import jax
import jax.numpy as jnp
from jax import lax
from jax.experimental import pallas as pl
from jax.experimental.pallas import tpu as pltpu
from jax.sharding import Mesh, PartitionSpec as P

ROWS = ("zh", "x", "c")
FEATS = ("y", "zl")
COLUMN = ("zh", "zl")
BF = jnp.bfloat16
F32 = jnp.float32
BAND = 32


def shift(value, axis, step):
    n = lax.axis_size(axis)
    return lax.ppermute(value, axis, [(i, (i + step) % n) for i in range(n)])


def flip(value, axis, bit):
    return lax.ppermute(value, axis, [(i, i ^ bit) for i in range(lax.axis_size(axis))])


def exchange(blocks, axis):
    return lax.all_to_all(blocks, axis, 0, 0, tiled=True)


def gather(value, axis):
    n = lax.axis_size(axis)
    return exchange(jnp.broadcast_to(value, (n, *value.shape)), axis)


def dot(a, b, over_a, over_b):
    return lax.dot_general(a, b, (((over_a,), (over_b,)), ((), ())), preferred_element_type=F32)


def call(kernel, outs, flops, place, *arrays):
    size = sum(a.size * a.dtype.itemsize for a in (*arrays, *outs))
    return pl.pallas_call(
        kernel,
        out_shape=outs,
        in_specs=[pl.BlockSpec(memory_space=pltpu.SMEM)] + [pl.BlockSpec(memory_space=pltpu.VMEM)] * len(arrays),
        out_specs=[pl.BlockSpec(memory_space=pltpu.VMEM)] * len(outs),
        cost_estimate=pl.CostEstimate(flops=flops, bytes_accessed=size, transcendentals=0),
        compiler_params=pltpu.CompilerParams(vmem_limit_bytes=32 * 2**20),
    )(place.reshape(1), *arrays)


def logits_kernel(place_ref, q_ref, p_ref, p_other_ref, out_ref):
    del place_ref
    n_zh = out_ref.shape[0]
    count = p_ref.shape[0]
    n_x = q_ref.shape[0] // n_zh // BAND
    for side, side_ref in enumerate((p_ref, p_other_ref)):
        block = dot(q_ref[...], side_ref[...], 1, 1)
        for x in range(n_x):
            for z in range(n_zh):
                at = (x * n_zh + z) * BAND
                out_ref[z, x * BAND : (x + 1) * BAND, side * count : (side + 1) * count] = block[at : at + BAND]


def passage_kernel(zl_ref, w_ref, far_w_ref, near_ref, far_ref, keep_ref, send_ref):
    _, count, width = keep_ref.shape
    n_zh, n_x = w_ref.shape[:2]
    order = [(z, x) for x in range(n_x) for z in range(n_zh)]
    w_near = jnp.concatenate([w_ref[z, x, :, :count] for z, x in order], axis=0)
    w_far = jnp.concatenate([far_w_ref[z, x] for z, x in order], axis=0)
    for i, flip in enumerate((0, 2, 1, 3)):
        at = pl.ds(pl.multiple_of((zl_ref[0] ^ flip) * width, width), width)
        block = dot(w_near, near_ref[:, at], 0, 0) + dot(w_far, far_ref[:, at], 0, 0)
        if i < 2:
            keep_ref[i] = block
        else:
            send_ref[i - 2] = block.astype(BF)


def spread_kernel(place_ref, in_ref, out_ref):
    del place_ref
    n, band, _ = out_ref.shape
    n_bands = in_ref.shape[0] // band
    for i in range(n):
        out_ref[i] = in_ref[pl.ds(i % n_bands * band, band), :]


def collect_kernel(place_ref, in_ref, out_ref):
    del place_ref
    n, band, width = in_ref.shape
    n_zl = out_ref.shape[2] // width
    for i in range(n):
        for x in range(out_ref.shape[0]):
            at = i // n_zl * band
            out_ref[x, at : at + band, i % n_zl * width : (i % n_zl + 1) * width] = in_ref[i]


def query_block(w_ref, p_ref, p_other_ref, x):
    count = p_ref.shape[0]
    rows = jnp.concatenate([w_ref[z, x] for z in range(w_ref.shape[0])], axis=0)
    return dot(rows[:, :count], p_ref[...], 1, 0) + dot(rows[:, count:], p_other_ref[...], 1, 0)


def query_kernel(x_ref, w_ref, p_ref, p_other_ref, send_ref):
    del x_ref
    for x in range(send_ref.shape[0]):
        send_ref[x] = query_block(w_ref, p_ref, p_other_ref, x).astype(BF)


def own_kernel(x_ref, w_ref, p_ref, p_other_ref, out_ref):
    out_ref[...] = query_block(w_ref, p_ref, p_other_ref, x_ref[0])


def total_kernel(x_ref, own_ref, moved_ref, out_ref):
    n_x, n_rows, strip = moved_ref.shape
    n_blocks, band, width = out_ref.shape
    n_zl = strip // width
    total = own_ref[...]
    for x in range(n_x):
        total = total + jnp.where(x_ref[0] == x, 0.0, moved_ref[x].astype(F32))
    for z in range(n_blocks // n_zl):
        for l in range(n_zl):
            out_ref[z * n_zl + l] = total[z * band : (z + 1) * band, l * width : (l + 1) * width].astype(BF)


def per_device(queries, passages, positive):
    rows, width = queries.shape
    count = passages.shape[0]
    n_x, n_y, n_zh, n_zl = (lax.axis_size(a) for a in ("x", "y", "zh", "zl"))
    strip = width * n_zl
    scale = 2.0 / math.sqrt(strip * n_y)
    band = rows // n_zl
    assert n_zh == n_y and band == BAND
    n_q = n_x * band
    n_half = band * n_zh * n_x
    x, y, zl = (lax.axis_index(a) for a in ("x", "y", "zl"))
    dev = lax.axis_index(ROWS)

    bands = jax.ShapeDtypeStruct((n_zh * n_zl, band, width), BF)
    spread = jax.ShapeDtypeStruct((n_x, n_zh * band, strip), BF)
    (mine,) = call(spread_kernel, [bands], 0, x, queries)
    (mine,) = call(collect_kernel, [spread], 0, x, exchange(mine, COLUMN))
    near = exchange(mine, "x").reshape(n_half, strip)

    p = jnp.zeros((count, strip), BF)
    for t in range(n_zl):
        block = passages if t == 0 else shift(passages, "zl", t)
        p = lax.dynamic_update_slice_in_dim(p, block, (zl - t) % n_zl * width, 1)
    p_other = shift(p, "c", 1)
    near, p = lax.optimization_barrier((near, p))
    far = shift(near, "c", 1)

    flops = 4 * n_half * count * strip
    (partial,) = call(
        logits_kernel, [jax.ShapeDtypeStruct((n_zh, n_q, 2 * count), F32)], flops, x, near, p, p_other
    )
    moved = exchange(partial, "y")
    logits = moved[0]
    for i in range(1, n_y):
        logits = logits + moved[i]
    logits = logits * scale

    top = jnp.max(logits, axis=1)
    exps = jnp.exp(logits - top[:, None])
    total = jnp.sum(exps, axis=1)
    own_pos = lax.dynamic_slice_in_dim(positive, zl * band, band).astype(F32)
    note = jnp.concatenate([top, total, jnp.pad(own_pos, (0, 128 - band))])
    notes = exchange(jnp.broadcast_to(note, (n_x * n_zh, note.shape[0])), ("x", "zh"))
    tops, totals = notes[:, :n_q], notes[:, n_q : 2 * n_q]
    pos = notes[:, 2 * n_q : 2 * n_q + band].reshape(n_x, n_zh, band)
    pos = lax.dynamic_index_in_dim(pos, y, 1, keepdims=False).reshape(n_q).astype(jnp.int32)
    peak = jnp.max(tops, axis=0)
    denom = jnp.sum(totals * jnp.exp(tops - peak), axis=0)
    factor = jnp.exp(top - peak) / denom
    columns = lax.broadcasted_iota(jnp.int32, (n_q, 2 * count), 1)
    columns = jnp.where(columns < count, columns + dev * count, columns - count + (dev ^ 1) * count)
    onehot = (columns == pos[:, None]).astype(F32)
    weights = (exps * factor[:, None] - onehot).astype(BF)
    weights = gather(weights, "y").reshape(n_zh, n_x, band, 2 * count)
    far_weights = shift(weights[..., count:], "c", 1)

    block = (n_zh * band, strip)
    (chip,) = call(query_kernel, [jax.ShapeDtypeStruct((n_x, *block), BF)], flops, x, weights, p, p_other)
    moved = exchange(chip, "x")
    (own,) = call(own_kernel, [jax.ShapeDtypeStruct(block, F32)], flops // n_x, x, weights, p, p_other)
    (back,) = call(total_kernel, [bands], 0, x, own, moved)

    pair = (2, count, width)
    keep, send = call(
        passage_kernel,
        [jax.ShapeDtypeStruct(pair, F32), jax.ShapeDtypeStruct(pair, BF)],
        flops, zl, weights, far_weights, near, far,
    )
    arrived = flip(send, "zl", 1)
    back, arrived = lax.optimization_barrier((back, arrived))
    passage_grad = keep[0] + arrived[0].astype(F32)
    passage_grad += flip((keep[1] + arrived[1].astype(F32)).astype(BF), "zl", 2).astype(F32)

    back = exchange(back, COLUMN).reshape(n_zh, rows, width)
    query_grad = jnp.sum(back.astype(F32), axis=0)
    return query_grad.astype(BF), passage_grad.astype(BF)


def solution(mesh):
    fine = Mesh(mesh.devices.reshape(4, 4, 4, 4, 2), FEATS + ROWS)
    in_specs = (P(ROWS, FEATS), P(ROWS, FEATS), P(ROWS))
    out_specs = (P(ROWS, FEATS), P(ROWS, FEATS))
    return jax.shard_map(per_device, mesh=fine, in_specs=in_specs, out_specs=out_specs, check_vma=False)
```

```python
import math

import jax
import jax.numpy as jnp
from jax import lax
from jax.experimental import pallas as pl
from jax.experimental.pallas import tpu as pltpu
from jax.sharding import Mesh, PartitionSpec as P

ROWS = ("zh", "x", "c")
FEATS = ("y", "zl")
COLUMN = ("zh", "zl")
BF = jnp.bfloat16
F32 = jnp.float32
BAND = 32
LONG = 10**10


def shift(value, axis, step):
    n = lax.axis_size(axis)
    return lax.ppermute(value, axis, [(i, (i + step) % n) for i in range(n)])


def flip(value, axis, bit):
    return lax.ppermute(value, axis, [(i, i ^ bit) for i in range(lax.axis_size(axis))])


def exchange(blocks, axis):
    return lax.all_to_all(blocks, axis, 0, 0, tiled=True)


def gather(value, axis):
    n = lax.axis_size(axis)
    return exchange(jnp.broadcast_to(value, (n, *value.shape)), axis)


def dot(a, b, over_a, over_b):
    return lax.dot_general(a, b, (((over_a,), (over_b,)), ((), ())), preferred_element_type=F32)


def call(kernel, outs, flops, place, *arrays):
    size = sum(a.size * a.dtype.itemsize for a in (*arrays, *outs))
    return pl.pallas_call(
        kernel,
        out_shape=outs,
        in_specs=[pl.BlockSpec(memory_space=pltpu.SMEM)] + [pl.BlockSpec(memory_space=pltpu.VMEM)] * len(arrays),
        out_specs=[pl.BlockSpec(memory_space=pltpu.VMEM)] * len(outs),
        cost_estimate=pl.CostEstimate(flops=flops, bytes_accessed=size, transcendentals=0),
        compiler_params=pltpu.CompilerParams(vmem_limit_bytes=32 * 2**20),
    )(place.reshape(1), *arrays)


def logits_kernel(place_ref, q_ref, p_ref, p_other_ref, out_ref):
    del place_ref
    n_zh = out_ref.shape[0]
    count = p_ref.shape[0]
    n_x = q_ref.shape[0] // n_zh // BAND
    for side, side_ref in enumerate((p_ref, p_other_ref)):
        block = dot(q_ref[...], side_ref[...], 1, 1)
        for x in range(n_x):
            for z in range(n_zh):
                at = (x * n_zh + z) * BAND
                out_ref[z, x * BAND : (x + 1) * BAND, side * count : (side + 1) * count] = block[at : at + BAND]


def passage_kernel(zl_ref, w_ref, far_w_ref, near_ref, far_ref, keep_ref, send_ref):
    _, count, width = keep_ref.shape
    n_zh, n_x = w_ref.shape[:2]
    order = [(z, x) for x in range(n_x) for z in range(n_zh)]
    w_near = jnp.concatenate([w_ref[z, x, :, :count] for z, x in order], axis=0)
    w_far = jnp.concatenate([far_w_ref[z, x] for z, x in order], axis=0)
    for i, flip in enumerate((0, 2, 1, 3)):
        at = pl.ds(pl.multiple_of((zl_ref[0] ^ flip) * width, width), width)
        block = dot(w_near, near_ref[:, at], 0, 0) + dot(w_far, far_ref[:, at], 0, 0)
        if i < 2:
            keep_ref[i] = block
        else:
            send_ref[i - 2] = block.astype(BF)


def pair_kernel(place_ref, keep_ref, arrived_ref, own_ref, send_ref):
    del place_ref
    own_ref[...] = keep_ref[0] + arrived_ref[0].astype(F32)
    send_ref[...] = (keep_ref[1] + arrived_ref[1].astype(F32)).astype(BF)


def spread_kernel(place_ref, in_ref, out_ref):
    del place_ref
    n, band, _ = out_ref.shape
    n_bands = in_ref.shape[0] // band
    for i in range(n):
        out_ref[i] = in_ref[pl.ds(i % n_bands * band, band), :]


def collect_kernel(place_ref, in_ref, out_ref):
    del place_ref
    n, band, width = in_ref.shape
    n_zl = out_ref.shape[2] // width
    for i in range(n):
        for x in range(out_ref.shape[0]):
            at = i // n_zl * band
            out_ref[x, at : at + band, i % n_zl * width : (i % n_zl + 1) * width] = in_ref[i]


def query_block(w_ref, p_ref, p_other_ref, x):
    count = p_ref.shape[0]
    rows = jnp.concatenate([w_ref[z, x] for z in range(w_ref.shape[0])], axis=0)
    return dot(rows[:, :count], p_ref[...], 1, 0) + dot(rows[:, count:], p_other_ref[...], 1, 0)


def query_kernel(x_ref, w_ref, p_ref, p_other_ref, send_ref):
    del x_ref
    for x in range(send_ref.shape[0]):
        send_ref[x] = query_block(w_ref, p_ref, p_other_ref, x).astype(BF)


def own_kernel(x_ref, w_ref, p_ref, p_other_ref, out_ref):
    out_ref[...] = query_block(w_ref, p_ref, p_other_ref, x_ref[0])


def total_kernel(x_ref, own_ref, moved_ref, out_ref):
    n_x, n_rows, strip = moved_ref.shape
    n_blocks, band, width = out_ref.shape
    n_zl = strip // width
    total = own_ref[...]
    for x in range(n_x):
        total = total + jnp.where(x_ref[0] == x, 0.0, moved_ref[x].astype(F32))
    for z in range(n_blocks // n_zl):
        for l in range(n_zl):
            out_ref[z * n_zl + l] = total[z * band : (z + 1) * band, l * width : (l + 1) * width].astype(BF)


def per_device(queries, passages, positive):
    rows, width = queries.shape
    count = passages.shape[0]
    n_x, n_y, n_zh, n_zl = (lax.axis_size(a) for a in ("x", "y", "zh", "zl"))
    strip = width * n_zl
    scale = 2.0 / math.sqrt(strip * n_y)
    band = rows // n_zl
    assert n_zh == n_y and band == BAND
    n_q = n_x * band
    n_half = band * n_zh * n_x
    x, y, zl = (lax.axis_index(a) for a in ("x", "y", "zl"))
    dev = lax.axis_index(ROWS)

    bands = jax.ShapeDtypeStruct((n_zh * n_zl, band, width), BF)
    spread = jax.ShapeDtypeStruct((n_x, n_zh * band, strip), BF)
    (mine,) = call(spread_kernel, [bands], 0, x, queries)
    (mine,) = call(collect_kernel, [spread], 0, x, exchange(mine, COLUMN))
    near = exchange(mine, "x").reshape(n_half, strip)

    p = jnp.zeros((count, strip), BF)
    for t in range(n_zl):
        block = passages if t == 0 else shift(passages, "zl", t)
        p = lax.dynamic_update_slice_in_dim(p, block, (zl - t) % n_zl * width, 1)
    p_other = shift(p, "c", 1)
    near, p = lax.optimization_barrier((near, p))
    far = shift(near, "c", 1)

    flops = 4 * n_half * count * strip
    (partial,) = call(
        logits_kernel, [jax.ShapeDtypeStruct((n_zh, n_q, 2 * count), F32)], flops, x, near, p, p_other
    )
    moved = exchange(partial, "y")
    logits = moved[0]
    for i in range(1, n_y):
        logits = logits + moved[i]
    logits = logits * scale

    top = jnp.max(logits, axis=1)
    exps = jnp.exp(logits - top[:, None])
    total = jnp.sum(exps, axis=1)
    own_pos = lax.dynamic_slice_in_dim(positive, zl * band, band).astype(F32)
    note = jnp.concatenate([top, total, jnp.pad(own_pos, (0, 128 - band))])
    notes = exchange(jnp.broadcast_to(note, (n_x * n_zh, note.shape[0])), ("x", "zh"))
    tops, totals = notes[:, :n_q], notes[:, n_q : 2 * n_q]
    pos = notes[:, 2 * n_q : 2 * n_q + band].reshape(n_x, n_zh, band)
    pos = lax.dynamic_index_in_dim(pos, y, 1, keepdims=False).reshape(n_q).astype(jnp.int32)
    peak = jnp.max(tops, axis=0)
    denom = jnp.sum(totals * jnp.exp(tops - peak), axis=0)
    factor = jnp.exp(top - peak) / denom
    columns = lax.broadcasted_iota(jnp.int32, (n_q, 2 * count), 1)
    columns = jnp.where(columns < count, columns + dev * count, columns - count + (dev ^ 1) * count)
    onehot = (columns == pos[:, None]).astype(F32)
    weights = (exps * factor[:, None] - onehot).astype(BF)
    weights = gather(weights, "y").reshape(n_zh, n_x, band, 2 * count)
    far_weights = shift(weights[..., count:], "c", 1)

    block = (n_zh * band, strip)
    (chip,) = call(query_kernel, [jax.ShapeDtypeStruct((n_x, *block), BF)], flops, x, weights, p, p_other)
    moved = exchange(chip, "x")
    (own,) = call(own_kernel, [jax.ShapeDtypeStruct(block, F32)], flops // n_x, x, weights, p, p_other)
    (back,) = call(total_kernel, [bands], 0, x, own, moved)

    pair = (2, count, width)
    keep, send = call(
        passage_kernel,
        [jax.ShapeDtypeStruct(pair, F32), jax.ShapeDtypeStruct(pair, BF)],
        flops, zl, weights, far_weights, near, far,
    )
    arrived = flip(send, "zl", 1)
    passage_grad, send = call(
        pair_kernel,
        [jax.ShapeDtypeStruct((count, width), F32), jax.ShapeDtypeStruct((count, width), BF)],
        LONG, zl, keep, arrived,
    )
    passage_grad += flip(send, "zl", 2).astype(F32)

    back = exchange(back, COLUMN).reshape(n_zh, rows, width)
    query_grad = jnp.sum(back.astype(F32), axis=0)
    return query_grad.astype(BF), passage_grad.astype(BF)


def solution(mesh):
    fine = Mesh(mesh.devices.reshape(4, 4, 4, 4, 2), FEATS + ROWS)
    in_specs = (P(ROWS, FEATS), P(ROWS, FEATS), P(ROWS))
    out_specs = (P(ROWS, FEATS), P(ROWS, FEATS))
    return jax.shard_map(per_device, mesh=fine, in_specs=in_specs, out_specs=out_specs, check_vma=False)
```

```python
import math

import jax
import jax.numpy as jnp
from jax import lax
from jax.experimental import pallas as pl
from jax.experimental.pallas import tpu as pltpu
from jax.sharding import Mesh, PartitionSpec as P

ROWS = ("zh", "x", "c")
FEATS = ("y", "zl")
COLUMN = ("zl", "zh")
BF = jnp.bfloat16
F32 = jnp.float32
BAND = 32
LONG = 10**10


def shift(value, axis, step):
    n = lax.axis_size(axis)
    return lax.ppermute(value, axis, [(i, (i + step) % n) for i in range(n)])


def flip(value, axis, bit):
    return lax.ppermute(value, axis, [(i, i ^ bit) for i in range(lax.axis_size(axis))])


def exchange(blocks, axis):
    return lax.all_to_all(blocks, axis, 0, 0, tiled=True)


def gather(value, axis):
    n = lax.axis_size(axis)
    return exchange(jnp.broadcast_to(value, (n, *value.shape)), axis)


def dot(a, b, over_a, over_b):
    return lax.dot_general(a, b, (((over_a,), (over_b,)), ((), ())), preferred_element_type=F32)


def call(kernel, outs, flops, place, *arrays):
    size = sum(a.size * a.dtype.itemsize for a in (*arrays, *outs))
    return pl.pallas_call(
        kernel,
        out_shape=outs,
        in_specs=[pl.BlockSpec(memory_space=pltpu.SMEM)] + [pl.BlockSpec(memory_space=pltpu.VMEM)] * len(arrays),
        out_specs=[pl.BlockSpec(memory_space=pltpu.VMEM)] * len(outs),
        cost_estimate=pl.CostEstimate(flops=flops, bytes_accessed=size, transcendentals=0),
        compiler_params=pltpu.CompilerParams(vmem_limit_bytes=32 * 2**20),
    )(place.reshape(1), *arrays)


def logits_kernel(place_ref, q_ref, p_ref, p_other_ref, out_ref):
    del place_ref
    n_zh = out_ref.shape[0]
    count = p_ref.shape[0]
    n_x = q_ref.shape[0] // n_zh // BAND
    for side, side_ref in enumerate((p_ref, p_other_ref)):
        block = dot(q_ref[...], side_ref[...], 1, 1)
        for x in range(n_x):
            for z in range(n_zh):
                at = (x * n_zh + z) * BAND
                out_ref[z, x * BAND : (x + 1) * BAND, side * count : (side + 1) * count] = block[at : at + BAND]


def passage_kernel(zl_ref, w_ref, far_w_ref, near_ref, far_ref, keep_ref, send_ref):
    _, count, width = keep_ref.shape
    n_zh, n_x = w_ref.shape[:2]
    order = [(z, x) for x in range(n_x) for z in range(n_zh)]
    w_near = jnp.concatenate([w_ref[z, x, :, :count] for z, x in order], axis=0)
    w_far = jnp.concatenate([far_w_ref[z, x] for z, x in order], axis=0)
    for i, flip in enumerate((0, 2, 1, 3)):
        at = pl.ds(pl.multiple_of((zl_ref[0] ^ flip) * width, width), width)
        block = dot(w_near, near_ref[:, at], 0, 0) + dot(w_far, far_ref[:, at], 0, 0)
        if i < 2:
            keep_ref[i] = block
        else:
            send_ref[i - 2] = block.astype(BF)


def pair_kernel(place_ref, keep_ref, arrived_ref, own_ref, send_ref):
    del place_ref
    own_ref[...] = keep_ref[0] + arrived_ref[0].astype(F32)
    send_ref[...] = (keep_ref[1] + arrived_ref[1].astype(F32)).astype(BF)


def spread_kernel(place_ref, in_ref, out_ref):
    del place_ref
    n, band, _ = out_ref.shape
    n_bands = in_ref.shape[0] // band
    for i in range(n):
        out_ref[i] = in_ref[pl.ds(i // (n // n_bands) * band, band), :]


def collect_kernel(place_ref, in_ref, out_ref):
    del place_ref
    n, band, width = in_ref.shape
    n_zl = out_ref.shape[2] // width
    for i in range(n):
        for x in range(out_ref.shape[0]):
            z, l = i % (n // n_zl), i // (n // n_zl)
            out_ref[x, z * band : (z + 1) * band, l * width : (l + 1) * width] = in_ref[i]


def query_block(w_ref, p_ref, p_other_ref, x):
    count = p_ref.shape[0]
    rows = jnp.concatenate([w_ref[z, x] for z in range(w_ref.shape[0])], axis=0)
    return dot(rows[:, :count], p_ref[...], 1, 0) + dot(rows[:, count:], p_other_ref[...], 1, 0)


def query_kernel(x_ref, w_ref, p_ref, p_other_ref, send_ref):
    del x_ref
    for x in range(send_ref.shape[0]):
        send_ref[x] = query_block(w_ref, p_ref, p_other_ref, x).astype(BF)


def own_kernel(x_ref, w_ref, p_ref, p_other_ref, out_ref):
    out_ref[...] = query_block(w_ref, p_ref, p_other_ref, x_ref[0])


def total_kernel(x_ref, own_ref, moved_ref, out_ref):
    n_x, n_rows, strip = moved_ref.shape
    n_blocks, band, width = out_ref.shape
    n_zl = strip // width
    total = own_ref[...]
    for x in range(n_x):
        total = total + jnp.where(x_ref[0] == x, 0.0, moved_ref[x].astype(F32))
    for z in range(n_blocks // n_zl):
        for l in range(n_zl):
            out_ref[l * (n_blocks // n_zl) + z] = total[z * band : (z + 1) * band, l * width : (l + 1) * width].astype(BF)


def per_device(queries, passages, positive):
    rows, width = queries.shape
    count = passages.shape[0]
    n_x, n_y, n_zh, n_zl = (lax.axis_size(a) for a in ("x", "y", "zh", "zl"))
    strip = width * n_zl
    scale = 2.0 / math.sqrt(strip * n_y)
    band = rows // n_zl
    assert n_zh == n_y and band == BAND
    n_q = n_x * band
    n_half = band * n_zh * n_x
    x, y, zl = (lax.axis_index(a) for a in ("x", "y", "zl"))
    dev = lax.axis_index(ROWS)

    bands = jax.ShapeDtypeStruct((n_zh * n_zl, band, width), BF)
    spread = jax.ShapeDtypeStruct((n_x, n_zh * band, strip), BF)
    (mine,) = call(spread_kernel, [bands], 0, x, queries)
    (mine,) = call(collect_kernel, [spread], 0, x, exchange(mine, COLUMN))
    near = exchange(mine, "x").reshape(n_half, strip)

    p = jnp.zeros((count, strip), BF)
    for t in range(n_zl):
        block = passages if t == 0 else shift(passages, "zl", t)
        p = lax.dynamic_update_slice_in_dim(p, block, (zl - t) % n_zl * width, 1)
    p_other = shift(p, "c", 1)
    near, p = lax.optimization_barrier((near, p))
    far = shift(near, "c", 1)

    flops = 4 * n_half * count * strip
    (partial,) = call(
        logits_kernel, [jax.ShapeDtypeStruct((n_zh, n_q, 2 * count), F32)], flops, x, near, p, p_other
    )
    moved = exchange(partial, "y")
    logits = moved[0]
    for i in range(1, n_y):
        logits = logits + moved[i]
    logits = logits * scale

    top = jnp.max(logits, axis=1)
    exps = jnp.exp(logits - top[:, None])
    total = jnp.sum(exps, axis=1)
    own_pos = lax.dynamic_slice_in_dim(positive, zl * band, band).astype(F32)
    note = jnp.concatenate([top, total, jnp.pad(own_pos, (0, 128 - band))])
    notes = exchange(jnp.broadcast_to(note, (n_x * n_zh, note.shape[0])), ("x", "zh"))
    tops, totals = notes[:, :n_q], notes[:, n_q : 2 * n_q]
    pos = notes[:, 2 * n_q : 2 * n_q + band].reshape(n_x, n_zh, band)
    pos = lax.dynamic_index_in_dim(pos, y, 1, keepdims=False).reshape(n_q).astype(jnp.int32)
    peak = jnp.max(tops, axis=0)
    denom = jnp.sum(totals * jnp.exp(tops - peak), axis=0)
    factor = jnp.exp(top - peak) / denom
    columns = lax.broadcasted_iota(jnp.int32, (n_q, 2 * count), 1)
    columns = jnp.where(columns < count, columns + dev * count, columns - count + (dev ^ 1) * count)
    onehot = (columns == pos[:, None]).astype(F32)
    weights = (exps * factor[:, None] - onehot).astype(BF)
    weights = gather(weights, "y").reshape(n_zh, n_x, band, 2 * count)
    far_weights = shift(weights[..., count:], "c", 1)

    block = (n_zh * band, strip)
    (chip,) = call(query_kernel, [jax.ShapeDtypeStruct((n_x, *block), BF)], flops, x, weights, p, p_other)
    moved = exchange(chip, "x")
    (own,) = call(own_kernel, [jax.ShapeDtypeStruct(block, F32)], flops // n_x, x, weights, p, p_other)
    (back,) = call(total_kernel, [bands], 0, x, own, moved)

    pair = (2, count, width)
    keep, send = call(
        passage_kernel,
        [jax.ShapeDtypeStruct(pair, F32), jax.ShapeDtypeStruct(pair, BF)],
        flops, zl, weights, far_weights, near, far,
    )
    arrived = flip(send, "zl", 1)
    passage_grad, send = call(
        pair_kernel,
        [jax.ShapeDtypeStruct((count, width), F32), jax.ShapeDtypeStruct((count, width), BF)],
        LONG, zl, keep, arrived,
    )
    passage_grad += flip(send, "zl", 2).astype(F32)

    back = exchange(back, COLUMN).reshape(n_zl, n_zh, band, width)
    query_grad = jnp.sum(back.astype(F32), axis=1).reshape(rows, width)
    return query_grad.astype(BF), passage_grad.astype(BF)


def solution(mesh):
    fine = Mesh(mesh.devices.reshape(4, 4, 4, 4, 2), FEATS + ROWS)
    in_specs = (P(ROWS, FEATS), P(ROWS, FEATS), P(ROWS))
    out_specs = (P(ROWS, FEATS), P(ROWS, FEATS))
    return jax.shard_map(per_device, mesh=fine, in_specs=in_specs, out_specs=out_specs, check_vma=False)
```

```python
import math

import jax
import jax.numpy as jnp
from jax import lax
from jax.experimental import pallas as pl
from jax.experimental.pallas import tpu as pltpu
from jax.sharding import Mesh, PartitionSpec as P

ROWS = ("zh", "x", "c")
FEATS = ("y", "zl")
COLUMN = ("zl", "zh")
BF = jnp.bfloat16
F32 = jnp.float32
BAND = 32
LONG = 10**10


def shift(value, axis, step):
    n = lax.axis_size(axis)
    return lax.ppermute(value, axis, [(i, (i + step) % n) for i in range(n)])


def flip(value, axis, bit):
    return lax.ppermute(value, axis, [(i, i ^ bit) for i in range(lax.axis_size(axis))])


def exchange(blocks, axis):
    return lax.all_to_all(blocks, axis, 0, 0, tiled=True)


def gather(value, axis):
    n = lax.axis_size(axis)
    return exchange(jnp.broadcast_to(value, (n, *value.shape)), axis)


def dot(a, b, over_a, over_b):
    return lax.dot_general(a, b, (((over_a,), (over_b,)), ((), ())), preferred_element_type=F32)


def call(kernel, outs, flops, place, *arrays):
    size = sum(a.size * a.dtype.itemsize for a in (*arrays, *outs))
    return pl.pallas_call(
        kernel,
        out_shape=outs,
        in_specs=[pl.BlockSpec(memory_space=pltpu.SMEM)] + [pl.BlockSpec(memory_space=pltpu.VMEM)] * len(arrays),
        out_specs=[pl.BlockSpec(memory_space=pltpu.VMEM)] * len(outs),
        cost_estimate=pl.CostEstimate(flops=flops, bytes_accessed=size, transcendentals=0),
        compiler_params=pltpu.CompilerParams(vmem_limit_bytes=32 * 2**20),
    )(place.reshape(1), *arrays)


def logits_kernel(place_ref, q_ref, p_ref, p_other_ref, out_ref):
    del place_ref
    n_zh = out_ref.shape[0]
    count = p_ref.shape[0]
    n_x = q_ref.shape[0] // n_zh // BAND
    for side, side_ref in enumerate((p_ref, p_other_ref)):
        block = dot(q_ref[...], side_ref[...], 1, 1)
        for x in range(n_x):
            for z in range(n_zh):
                at = (x * n_zh + z) * BAND
                out_ref[z, x * BAND : (x + 1) * BAND, side * count : (side + 1) * count] = block[at : at + BAND]


def passage_kernel(zl_ref, w_ref, far_w_ref, near_ref, far_ref, keep_ref, send_ref):
    _, count, width = keep_ref.shape
    n_zh, n_x = w_ref.shape[:2]
    order = [(z, x) for x in range(n_x) for z in range(n_zh)]
    w_near = jnp.concatenate([w_ref[z, x, :, :count] for z, x in order], axis=0)
    w_far = jnp.concatenate([far_w_ref[z, x] for z, x in order], axis=0)
    for i, flip in enumerate((0, 1, 2, 3)):
        at = pl.ds(pl.multiple_of((zl_ref[0] ^ flip) * width, width), width)
        block = dot(w_near, near_ref[:, at], 0, 0) + dot(w_far, far_ref[:, at], 0, 0)
        if i < 2:
            keep_ref[i] = block
        else:
            send_ref[i - 2] = block.astype(BF)


def pair_kernel(place_ref, keep_ref, arrived_ref, own_ref, send_ref):
    del place_ref
    own_ref[...] = keep_ref[0] + arrived_ref[0].astype(F32)
    send_ref[...] = (keep_ref[1] + arrived_ref[1].astype(F32)).astype(BF)


def spread_kernel(place_ref, in_ref, out_ref):
    del place_ref
    n, band, _ = out_ref.shape
    n_bands = in_ref.shape[0] // band
    for i in range(n):
        out_ref[i] = in_ref[pl.ds(i // (n // n_bands) * band, band), :]


def collect_kernel(place_ref, in_ref, out_ref):
    del place_ref
    n, band, width = in_ref.shape
    n_zl = out_ref.shape[2] // width
    for i in range(n):
        for x in range(out_ref.shape[0]):
            z, l = i % (n // n_zl), i // (n // n_zl)
            out_ref[x, z * band : (z + 1) * band, l * width : (l + 1) * width] = in_ref[i]


def query_block(w_ref, p_ref, p_other_ref, x):
    count = p_ref.shape[0]
    rows = jnp.concatenate([w_ref[z, x] for z in range(w_ref.shape[0])], axis=0)
    return dot(rows[:, :count], p_ref[...], 1, 0) + dot(rows[:, count:], p_other_ref[...], 1, 0)


def query_kernel(x_ref, w_ref, p_ref, p_other_ref, send_ref):
    del x_ref
    for x in range(send_ref.shape[0]):
        send_ref[x] = query_block(w_ref, p_ref, p_other_ref, x).astype(BF)


def own_kernel(x_ref, w_ref, p_ref, p_other_ref, out_ref):
    out_ref[...] = query_block(w_ref, p_ref, p_other_ref, x_ref[0])


def total_kernel(x_ref, own_ref, moved_ref, out_ref):
    n_x, n_rows, strip = moved_ref.shape
    n_blocks, band, width = out_ref.shape
    n_zl = strip // width
    total = own_ref[...]
    for x in range(n_x):
        total = total + jnp.where(x_ref[0] == x, 0.0, moved_ref[x].astype(F32))
    for z in range(n_blocks // n_zl):
        for l in range(n_zl):
            out_ref[l * (n_blocks // n_zl) + z] = total[z * band : (z + 1) * band, l * width : (l + 1) * width].astype(BF)


def per_device(queries, passages, positive):
    rows, width = queries.shape
    count = passages.shape[0]
    n_x, n_y, n_zh, n_zl = (lax.axis_size(a) for a in ("x", "y", "zh", "zl"))
    strip = width * n_zl
    scale = 2.0 / math.sqrt(strip * n_y)
    band = rows // n_zl
    assert n_zh == n_y and band == BAND
    n_q = n_x * band
    n_half = band * n_zh * n_x
    x, y, zl = (lax.axis_index(a) for a in ("x", "y", "zl"))
    dev = lax.axis_index(ROWS)

    bands = jax.ShapeDtypeStruct((n_zh * n_zl, band, width), BF)
    spread = jax.ShapeDtypeStruct((n_x, n_zh * band, strip), BF)
    (mine,) = call(spread_kernel, [bands], 0, x, queries)
    (mine,) = call(collect_kernel, [spread], 0, x, exchange(mine, COLUMN))
    near = exchange(mine, "x").reshape(n_half, strip)

    p = jnp.zeros((count, strip), BF)
    for t in range(n_zl):
        block = passages if t == 0 else shift(passages, "zl", t)
        p = lax.dynamic_update_slice_in_dim(p, block, (zl - t) % n_zl * width, 1)
    p_other = shift(p, "c", 1)
    near, p = lax.optimization_barrier((near, p))
    far = shift(near, "c", 1)

    flops = 4 * n_half * count * strip
    (partial,) = call(
        logits_kernel, [jax.ShapeDtypeStruct((n_zh, n_q, 2 * count), F32)], flops, x, near, p, p_other
    )
    moved = exchange(partial, "y")
    logits = moved[0]
    for i in range(1, n_y):
        logits = logits + moved[i]
    logits = logits * scale

    top = jnp.max(logits, axis=1)
    exps = jnp.exp(logits - top[:, None])
    total = jnp.sum(exps, axis=1)
    own_pos = lax.dynamic_slice_in_dim(positive, zl * band, band).astype(F32)
    note = jnp.concatenate([top, total, jnp.pad(own_pos, (0, 128 - band))])
    notes = exchange(jnp.broadcast_to(note, (n_x * n_zh, note.shape[0])), ("x", "zh"))
    tops, totals = notes[:, :n_q], notes[:, n_q : 2 * n_q]
    pos = notes[:, 2 * n_q : 2 * n_q + band].reshape(n_x, n_zh, band)
    pos = lax.dynamic_index_in_dim(pos, y, 1, keepdims=False).reshape(n_q).astype(jnp.int32)
    peak = jnp.max(tops, axis=0)
    denom = jnp.sum(totals * jnp.exp(tops - peak), axis=0)
    factor = jnp.exp(top - peak) / denom
    columns = lax.broadcasted_iota(jnp.int32, (n_q, 2 * count), 1)
    columns = jnp.where(columns < count, columns + dev * count, columns - count + (dev ^ 1) * count)
    onehot = (columns == pos[:, None]).astype(F32)
    weights = (exps * factor[:, None] - onehot).astype(BF)
    weights = gather(weights, "y").reshape(n_zh, n_x, band, 2 * count)
    far_weights = shift(weights[..., count:], "c", 1)

    block = (n_zh * band, strip)
    (chip,) = call(query_kernel, [jax.ShapeDtypeStruct((n_x, *block), BF)], flops, x, weights, p, p_other)
    moved = exchange(chip, "x")
    (own,) = call(own_kernel, [jax.ShapeDtypeStruct(block, F32)], flops // n_x, x, weights, p, p_other)
    (back,) = call(total_kernel, [bands], 0, x, own, moved)

    pair = (2, count, width)
    keep, send = call(
        passage_kernel,
        [jax.ShapeDtypeStruct(pair, F32), jax.ShapeDtypeStruct(pair, BF)],
        flops, zl, weights, far_weights, near, far,
    )
    arrived = flip(send, "zl", 2)
    passage_grad, send = call(
        pair_kernel,
        [jax.ShapeDtypeStruct((count, width), F32), jax.ShapeDtypeStruct((count, width), BF)],
        LONG, zl, keep, arrived,
    )
    passage_grad += flip(send, "zl", 1).astype(F32)

    back = exchange(back, COLUMN).reshape(n_zl, n_zh, band, width)
    query_grad = jnp.sum(back.astype(F32), axis=1).reshape(rows, width)
    return query_grad.astype(BF), passage_grad.astype(BF)


def solution(mesh):
    fine = Mesh(mesh.devices.reshape(4, 4, 4, 4, 2), FEATS + ROWS)
    in_specs = (P(ROWS, FEATS), P(ROWS, FEATS), P(ROWS))
    out_specs = (P(ROWS, FEATS), P(ROWS, FEATS))
    return jax.shard_map(per_device, mesh=fine, in_specs=in_specs, out_specs=out_specs, check_vma=False)
```

```python
import math

import jax
import jax.numpy as jnp
from jax import lax
from jax.experimental import pallas as pl
from jax.experimental.pallas import tpu as pltpu
from jax.sharding import Mesh, PartitionSpec as P

ROWS = ("zh", "x", "c")
FEATS = ("y", "zl")
COLUMN = ("zl", "zh")
BF = jnp.bfloat16
F32 = jnp.float32
BAND = 32
LONG = 10**10


def shift(value, axis, step):
    n = lax.axis_size(axis)
    return lax.ppermute(value, axis, [(i, (i + step) % n) for i in range(n)])


def flip(value, axis, bit):
    return lax.ppermute(value, axis, [(i, i ^ bit) for i in range(lax.axis_size(axis))])


def exchange(blocks, axis):
    return lax.all_to_all(blocks, axis, 0, 0, tiled=True)


def gather(value, axis):
    n = lax.axis_size(axis)
    return exchange(jnp.broadcast_to(value, (n, *value.shape)), axis)


def dot(a, b, over_a, over_b):
    return lax.dot_general(a, b, (((over_a,), (over_b,)), ((), ())), preferred_element_type=F32)


def call(kernel, outs, flops, place, *arrays):
    size = sum(a.size * a.dtype.itemsize for a in (*arrays, *outs))
    return pl.pallas_call(
        kernel,
        out_shape=outs,
        in_specs=[pl.BlockSpec(memory_space=pltpu.SMEM)] + [pl.BlockSpec(memory_space=pltpu.VMEM)] * len(arrays),
        out_specs=[pl.BlockSpec(memory_space=pltpu.VMEM)] * len(outs),
        cost_estimate=pl.CostEstimate(flops=flops, bytes_accessed=size, transcendentals=0),
        compiler_params=pltpu.CompilerParams(vmem_limit_bytes=32 * 2**20),
    )(place.reshape(1), *arrays)


def logits_kernel(place_ref, q_ref, p_ref, p_other_ref, out_ref):
    del place_ref
    n_zh = out_ref.shape[0]
    count = p_ref.shape[0]
    n_x = q_ref.shape[0] // n_zh // BAND
    for side, side_ref in enumerate((p_ref, p_other_ref)):
        block = dot(q_ref[...], side_ref[...], 1, 1)
        for x in range(n_x):
            for z in range(n_zh):
                at = (x * n_zh + z) * BAND
                out_ref[z, x * BAND : (x + 1) * BAND, side * count : (side + 1) * count] = block[at : at + BAND]


def passage_kernel(zl_ref, w_ref, far_w_ref, near_ref, far_ref, keep_ref, send_ref):
    _, count, width = keep_ref.shape
    n_zh, n_x = w_ref.shape[:2]
    order = [(z, x) for x in range(n_x) for z in range(n_zh)]
    w_near = jnp.concatenate([w_ref[z, x, :, :count] for z, x in order], axis=0)
    w_far = jnp.concatenate([far_w_ref[z, x] for z, x in order], axis=0)
    for i, flip in enumerate((0, 2, 1, 3)):
        at = pl.ds(pl.multiple_of((zl_ref[0] ^ flip) * width, width), width)
        block = dot(w_near, near_ref[:, at], 0, 0) + dot(w_far, far_ref[:, at], 0, 0)
        if i < 2:
            keep_ref[i] = block
        else:
            send_ref[i - 2] = block.astype(BF)


def pair_kernel(place_ref, keep_ref, arrived_ref, own_ref, send_ref):
    del place_ref
    own_ref[...] = keep_ref[0] + arrived_ref[0].astype(F32)
    send_ref[...] = (keep_ref[1] + arrived_ref[1].astype(F32)).astype(BF)


def collect_kernel(place_ref, in_ref, out_ref):
    del place_ref
    n, band, width = in_ref.shape
    n_zl = out_ref.shape[2] // width
    for i in range(n):
        for x in range(out_ref.shape[0]):
            z, l = i % (n // n_zl), i // (n // n_zl)
            out_ref[x, z * band : (z + 1) * band, l * width : (l + 1) * width] = in_ref[i]


def query_block(w_ref, p_ref, p_other_ref, x):
    count = p_ref.shape[0]
    rows = jnp.concatenate([w_ref[z, x] for z in range(w_ref.shape[0])], axis=0)
    return dot(rows[:, :count], p_ref[...], 1, 0) + dot(rows[:, count:], p_other_ref[...], 1, 0)


def query_kernel(x_ref, w_ref, p_ref, p_other_ref, send_ref):
    del x_ref
    for x in range(send_ref.shape[0]):
        send_ref[x] = query_block(w_ref, p_ref, p_other_ref, x).astype(BF)


def own_kernel(x_ref, w_ref, p_ref, p_other_ref, out_ref):
    out_ref[...] = query_block(w_ref, p_ref, p_other_ref, x_ref[0])


def total_kernel(x_ref, own_ref, moved_ref, out_ref):
    n_x, n_rows, strip = moved_ref.shape
    n_blocks, band, width = out_ref.shape
    n_zl = strip // width
    total = own_ref[...]
    for x in range(n_x):
        total = total + jnp.where(x_ref[0] == x, 0.0, moved_ref[x].astype(F32))
    for z in range(n_blocks // n_zl):
        for l in range(n_zl):
            out_ref[l * (n_blocks // n_zl) + z] = total[z * band : (z + 1) * band, l * width : (l + 1) * width].astype(BF)


def per_device(queries, passages, positive):
    rows, width = queries.shape
    count = passages.shape[0]
    n_x, n_y, n_zh, n_zl = (lax.axis_size(a) for a in ("x", "y", "zh", "zl"))
    strip = width * n_zl
    scale = 2.0 / math.sqrt(strip * n_y)
    band = rows // n_zl
    assert n_zh == n_y and band == BAND
    n_q = n_x * band
    n_half = band * n_zh * n_x
    x, y, zl = (lax.axis_index(a) for a in ("x", "y", "zl"))
    dev = lax.axis_index(ROWS)

    bands = jax.ShapeDtypeStruct((n_zh * n_zl, band, width), BF)
    spread = jax.ShapeDtypeStruct((n_x, n_zh * band, strip), BF)
    mine = jnp.broadcast_to(queries.reshape(n_zl, 1, band, width), (n_zl, n_zh, band, width)).reshape(bands.shape)
    (mine,) = call(collect_kernel, [spread], 0, x, exchange(mine, COLUMN))
    near = exchange(mine, "x").reshape(n_half, strip)

    p = jnp.zeros((count, strip), BF)
    for t in range(n_zl):
        block = passages if t == 0 else shift(passages, "zl", t)
        p = lax.dynamic_update_slice_in_dim(p, block, (zl - t) % n_zl * width, 1)
    p_other = shift(p, "c", 1)
    near, p = lax.optimization_barrier((near, p))
    far = shift(near, "c", 1)

    flops = 4 * n_half * count * strip
    (partial,) = call(
        logits_kernel, [jax.ShapeDtypeStruct((n_zh, n_q, 2 * count), F32)], flops, x, near, p, p_other
    )
    moved = exchange(partial, "y")
    logits = moved[0]
    for i in range(1, n_y):
        logits = logits + moved[i]
    logits = logits * scale

    top = jnp.max(logits, axis=1)
    exps = jnp.exp(logits - top[:, None])
    total = jnp.sum(exps, axis=1)
    own_pos = lax.dynamic_slice_in_dim(positive, zl * band, band).astype(F32)
    note = jnp.concatenate([top, total, jnp.pad(own_pos, (0, 128 - band))])
    notes = exchange(jnp.broadcast_to(note, (n_x * n_zh, note.shape[0])), ("x", "zh"))
    tops, totals = notes[:, :n_q], notes[:, n_q : 2 * n_q]
    pos = notes[:, 2 * n_q : 2 * n_q + band].reshape(n_x, n_zh, band)
    pos = lax.dynamic_index_in_dim(pos, y, 1, keepdims=False).reshape(n_q).astype(jnp.int32)
    peak = jnp.max(tops, axis=0)
    denom = jnp.sum(totals * jnp.exp(tops - peak), axis=0)
    factor = jnp.exp(top - peak) / denom
    columns = lax.broadcasted_iota(jnp.int32, (n_q, 2 * count), 1)
    columns = jnp.where(columns < count, columns + dev * count, columns - count + (dev ^ 1) * count)
    onehot = (columns == pos[:, None]).astype(F32)
    weights = (exps * factor[:, None] - onehot).astype(BF)
    weights = gather(weights, "y").reshape(n_zh, n_x, band, 2 * count)
    far_weights = shift(weights[..., count:], "c", 1)

    block = (n_zh * band, strip)
    (chip,) = call(query_kernel, [jax.ShapeDtypeStruct((n_x, *block), BF)], flops, x, weights, p, p_other)
    moved = exchange(chip, "x")
    (own,) = call(own_kernel, [jax.ShapeDtypeStruct(block, F32)], flops // n_x, x, weights, p, p_other)
    (back,) = call(total_kernel, [bands], 0, x, own, moved)

    pair = (2, count, width)
    keep, send = call(
        passage_kernel,
        [jax.ShapeDtypeStruct(pair, F32), jax.ShapeDtypeStruct(pair, BF)],
        flops, zl, weights, far_weights, near, far,
    )
    arrived = flip(send, "zl", 1)
    passage_grad, send = call(
        pair_kernel,
        [jax.ShapeDtypeStruct((count, width), F32), jax.ShapeDtypeStruct((count, width), BF)],
        LONG, zl, keep, arrived,
    )
    passage_grad += flip(send, "zl", 2).astype(F32)

    back = exchange(back, COLUMN).reshape(n_zl, n_zh, band, width)
    query_grad = jnp.sum(back.astype(F32), axis=1).reshape(rows, width)
    return query_grad.astype(BF), passage_grad.astype(BF)


def solution(mesh):
    fine = Mesh(mesh.devices.reshape(4, 4, 4, 4, 2), FEATS + ROWS)
    in_specs = (P(ROWS, FEATS), P(ROWS, FEATS), P(ROWS))
    out_specs = (P(ROWS, FEATS), P(ROWS, FEATS))
    return jax.shard_map(per_device, mesh=fine, in_specs=in_specs, out_specs=out_specs, check_vma=False)
```
